512 devices in a mesh: ev: 16 (over y_hi, x, core), cuts: 32 (over z, y_lo).
Axes of the slice: x: 4, y: 4 (y_hi: 2, y_lo: 2; y = y_hi * 2 + y_lo), z: 16, core: 2. Of those that a mesh axis runs over, the one named last changes fastest.
Arguments:
- kernels: float32 [16, 3, 32, 262144], P('ev', None, 'cuts')
- coords: float32 [3, 32, 262144], P(None, 'cuts', 'ev')
- neighbours: int32 [32, 2048, 9], P('cuts', 'ev'), may hold values from -1 to 389, as said below
Outputs:
- smoothed: float32 [3, 32, 262144], P(None, 'cuts', 'ev')
- irls_weights: float32 [3, 32, 262144], P(None, 'cuts', 'ev')
The draws below stay inside these ranges and needn't reach their ends.
Inputs may be any that keep to these rules, and one draw needn't show every extreme that they name: `neighbours`: each tile's nine slots name tiles among the 3 by (130) block around its device's tiles (the same and the two neighbouring slices, one tile beyond each end of the device's run), padded with -1; the tile's own slot (slot 4) is never -1 and no slot names a tile outside the mesh.
All inputs are finite; a program needn't handle non-finite values.
Results may differ from the reference program's by a relative error of at most 0.0003.
Values sent between devices are 32-bit elements; how exact they have to be, the bound alone decides.
A program may use at most 64 MiB of HBM per device.

```python
import jax
import jax.numpy as jnp
from jax import lax

K = 3
TILE = 128
NB = 9
TD = 128
EVENTS = 16
SLICES = 32
G = 2048
PTS_SLICE = 262144
N_EV = 16


def draw_kernels(key, part):
    key = jax.random.fold_in(key, 1)
    shape = (EVENTS, K, SLICES, PTS_SLICE)
    place = jnp.arange(SLICES, dtype=jnp.float32)
    rise = (0.6 + 1.2 * place / max(SLICES - 1, 1)).reshape(1, 1, SLICES, 1)
    return (jax.random.normal(key, shape, jnp.float32) * rise).astype(jnp.float32)


def draw_coords(key, part):
    key = jax.random.fold_in(key, 2)
    jitter = jax.random.uniform(key, (3, SLICES, PTS_SLICE), jnp.float32)
    slice_pos = jnp.broadcast_to(jnp.arange(SLICES, dtype=jnp.float32)[:, None], (SLICES, PTS_SLICE))
    tile_pos = jnp.broadcast_to((jnp.arange(PTS_SLICE) // TILE).astype(jnp.float32)[None, :], (SLICES, PTS_SLICE))
    base = jnp.stack([slice_pos, tile_pos, jnp.zeros((SLICES, PTS_SLICE), jnp.float32)])
    return (base + jitter).astype(jnp.float32)


def draw_neighbours(key, part):
    key = jax.random.fold_in(key, 3)
    slot = jnp.arange(NB, dtype=jnp.int32)[None, None, :]
    row = slot // 3
    col = slot % 3
    slice_id = jnp.arange(SLICES, dtype=jnp.int32)[:, None, None]
    tile_id = jnp.arange(G, dtype=jnp.int32)[None, :, None]
    within = tile_id % TD
    value = row * (TD + 2) + within + col
    inside = (slice_id + row - 1 >= 0) & (slice_id + row - 1 < SLICES) & (tile_id + col - 1 >= 0) & (tile_id + col - 1 < G)
    keep = (jax.random.randint(key, (SLICES, G, NB), 0, 4) > 0) | (slot == 4)
    return jnp.where(inside & keep, value, -1).astype(jnp.int32)


def setup_inputs(seed: int = 0) -> dict:
    streams_of = jax.random.split(jax.random.key(seed), 4)
    return {
        "kernels": draw_kernels(jax.random.fold_in(streams_of[3], 71), 0),
        "coords": draw_coords(jax.random.fold_in(streams_of[3], 71), 0),
        "neighbours": draw_neighbours(jax.random.fold_in(streams_of[3], 71), 0),
    }


def smooth_block(own_x, grid, ids):
    count = grid.shape[0] - 3
    tiles = ids.shape[0]
    group = 4
    xs = jnp.transpose(own_x.reshape(3, tiles // group, group, 128), (1, 0, 2, 3))
    ids_grouped = ids.reshape(tiles // group, group, ids.shape[1])

    def one(pair):
        here, idx = pair
        safe = jnp.maximum(idx, 0)
        valid = (idx >= 0).astype(jnp.float32)
        near = jnp.take(grid, safe.reshape(-1), axis=1).reshape(grid.shape[0], group, idx.shape[1], 128)
        dist = jnp.zeros((group, 128, idx.shape[1], 128), jnp.float32)
        for axis_id in range(3):
            diff = here[axis_id][:, :, None, None] - near[count + axis_id][:, None, :, :]
            dist = dist + diff * diff
        weights = jnp.exp(dist * (-1.0 / 0.72)) * valid[:, None, :, None]
        numer = jnp.einsum('tpsq,ktsq->ktp', weights, near[:count], precision=lax.Precision.HIGHEST)
        denom = lax.optimization_barrier(jnp.sum(weights, axis=(2, 3)))
        return numer / denom[None]
    out = lax.map(one, (xs, ids_grouped))
    return jnp.transpose(out, (1, 0, 2, 3)).reshape(out.shape[1], tiles, 128)

def reference(kernels, coords, neighbours):
    summed = lax.optimization_barrier(jnp.sum(kernels, axis=0))
    stacked = jnp.concatenate([summed, coords], axis=0).reshape(K + 3, SLICES, G, TILE)
    padded = jnp.pad(stacked, ((0, 0), (1, 1), (1, 1), (0, 0)))
    grid = padded.reshape(K + 3, (SLICES + 2) * (G + 2), TILE)

    def block(index):
        slice_id = (index // N_EV).astype(jnp.int32)
        part_id = (index % N_EV).astype(jnp.int32)
        start = (part_id * TD).astype(jnp.int32)
        own_x = lax.dynamic_slice(coords, (jnp.int32(0), slice_id, (start * TILE).astype(jnp.int32)), (3, 1, TD * TILE)).reshape(3, TD, TILE)
        local_ids = lax.dynamic_slice(neighbours, (slice_id, start, jnp.int32(0)), (1, TD, NB))[0]
        row = local_ids // (TD + 2)
        col = local_ids % (TD + 2)
        global_ids = (slice_id + row) * (G + 2) + start + col
        global_ids = jnp.where(local_ids >= 0, global_ids, -1).astype(jnp.int32)
        return smooth_block(own_x, grid, global_ids)
    blocks = lax.map(block, jnp.arange(SLICES * N_EV, dtype=jnp.int32))
    blocks = blocks.reshape(SLICES, N_EV, K, TD, TILE)
    smoothed = jnp.transpose(blocks, (2, 0, 1, 3, 4)).reshape(K, SLICES, PTS_SLICE)
    spread = jnp.sqrt(smoothed * smoothed + 0.01)
    lp_total = jnp.sum(spread)
    irls_weights = lp_total / (K * SLICES * PTS_SLICE) / spread
    return (smoothed, irls_weights)
```

```python
import functools
import jax
import jax.numpy as jnp
from jax import lax
from jax.experimental import pallas as pl
from jax.experimental.pallas import tpu as pltpu
from jax.sharding import PartitionSpec as P

MESH = pl.DeviceIdType.MESH
f32 = jnp.float32


def exchange(pieces, with_halo, cuts, d, x_ref, vg, xg, vcorner, xcorner,
             mine, other, x1, x2, yb, loc_sem, s0, r0, s1, r1, s2, r2, s3, r3, sh, rh):
    ev = lax.axis_index("ev")
    cut = lax.axis_index("cuts")
    core = lax.rem(ev, 2)
    x = lax.rem(lax.div(ev, 2), 4)
    yh = lax.div(ev, 8)

    def at(y_, x_, c_):
        return (y_ * 8 + x_ * 2 + c_, cut)

    xp, xm, xo = lax.rem(x + 1, 4), lax.rem(x + 3, 4), lax.rem(x + 2, 4)
    twin = at(yh, x, 1 - core)
    right, left = at(yh, xp, core), at(yh, xm, core)
    across = at(1 - yh, x, core)

    rel = [(0, -1), (0, 1)] + [(de, dc) for de in (-1, 1) for dc in (-1, 0, 1)] if with_halo else []

    def exists(de, dc):
        ok = jnp.bool_(True)
        if de: ok = ok & (ev + de >= 0) & (ev + de < 16)
        if dc: ok = ok & (cut + dc >= 0) & (cut + dc < cuts)
        return ok

    barrier = pltpu.get_barrier_semaphore()
    for dev in (twin, right, left, across):
        pl.semaphore_signal(barrier, inc=1, device_id=dev, device_id_type=MESH)
    for de, dc in rel:
        @pl.when(exists(de, dc))
        def _(de=de, dc=dc):
            pl.semaphore_signal(barrier, inc=1, device_id=(ev + de, cut + dc), device_id_type=MESH)
    expect = 4
    for de, dc in rel:
        expect = expect + exists(de, dc).astype(jnp.int32)

    n = len(pieces)
    width = [b - a for a, b in pieces]
    rows = [pl.ds(a, b - a) for a, b in pieces]
    ha = [pl.ds(a, (b - a) // 2) for a, b in pieces]
    hb = [pl.ds(a + (b - a) // 2, (b - a) // 2) for a, b in pieces]

    locs = []
    for p in range(n):
        c = pltpu.make_async_copy(d.at[:, :, :, core, rows[p]], mine.at[:, :, :, rows[p]], loc_sem.at[p])
        c.start()
        locs.append(c)
    pl.semaphore_wait(barrier, expect)

    def remote(src, dst, ss, rs, dev):
        c = pltpu.make_async_remote_copy(src_ref=src, dst_ref=dst, send_sem=ss, recv_sem=rs,
                                         device_id=dev, device_id_type=MESH)
        c.start()
        return c

    def halo(src, full, corner, base):
        for i, (de, dc) in enumerate(rel):
            if de == 0:
                s, t = src, full.at[1 - dc]
            else:
                s = src.at[:, pl.ds(120 if de > 0 else 0, 8)]
                t = corner.at[1 - dc, 0 if de > 0 else 1]
            c = pltpu.make_async_remote_copy(src_ref=s, dst_ref=t, send_sem=sh.at[base + i], recv_sem=rh.at[base + i],
                                             device_id=(ev + de, cut + dc), device_id_type=MESH)
            pl.when(exists(de, dc))(c.start)

    def halo_wait(src, full, corner, base):
        for i, (de, dc) in enumerate(rel):
            if de == 0:
                s, t = src, full.at[1 - dc]
            else:
                s = src.at[:, pl.ds(120 if de > 0 else 0, 8)]
                t = corner.at[1 - dc, 0 if de > 0 else 1]
            c = pltpu.make_async_remote_copy(src_ref=s, dst_ref=t, send_sem=sh.at[base + i], recv_sem=rh.at[base + i],
                                             device_id=(ev + de, cut + dc), device_id_type=MESH)
            pl.when(exists(de, dc))(c.wait_send)
            pl.when(exists(-de, -dc))(c.wait_recv)

    order = [xo, xp, xm, x]
    c0 = {}
    for p in range(n):
        for i, xx in enumerate(order):
            c0[p, i] = remote(d.at[:, :, xx, 1 - core, rows[p]], other.at[:, :, xx, rows[p]],
                              s0.at[p * 4 + i], r0.at[p * 4 + i], twin)
    if with_halo:
        halo(x_ref, xg, xcorner, 8)
    c1 = {}
    for p in range(n):
        locs[p].wait()
        c0[p, 0].wait_recv()
        mine[:, :, xo, rows[p]] += other[:, :, xo, rows[p]]
        c1[p, 0] = remote(mine.at[:, :, xo, ha[p]], x1.at[0, :, :, pl.ds(pieces[p][0] // 2, width[p] // 2)],
                          s1.at[2 * p], r1.at[2 * p], right)
        c1[p, 1] = remote(mine.at[:, :, xo, hb[p]], x1.at[1, :, :, pl.ds(pieces[p][0] // 2, width[p] // 2)],
                          s1.at[2 * p + 1], r1.at[2 * p + 1], left)
    c2 = {}
    for p in range(n):
        for side, xx, half in ((0, xp, ha[p]), (1, xm, hb[p])):
            c0[p, 1 + side].wait_recv()
            mine[:, :, xx, rows[p]] += other[:, :, xx, rows[p]]
            c1[p, side].wait_recv()
            mine[:, :, xx, half] += x1[side, :, :, pl.ds(pieces[p][0] // 2, width[p] // 2)]
            c2[p, side] = remote(mine.at[:, :, xx, rows[p]], x2.at[side, :, :, rows[p]],
                                 s2.at[2 * p + side], r2.at[2 * p + side], right if side == 0 else left)
    c3 = {}
    for p in range(n):
        c0[p, 3].wait_recv()
        mine[:, :, x, rows[p]] += other[:, :, x, rows[p]]
        for side in (0, 1):
            c2[p, side].wait_recv()
            mine[:, :, x, rows[p]] += x2[side, :, :, rows[p]]
        c3[p] = remote(mine.at[:, 1 - yh, x, rows[p]], yb.at[:, rows[p]], s3.at[p], r3.at[p], across)
    for p in range(n):
        c3[p].wait_recv()
        vg[1, :, rows[p]] = mine[:, yh, x, rows[p]] + yb[:, rows[p]]
    if with_halo:
        halo(vg.at[1], vg, vcorner, 0)
        xg[1] = x_ref[...]
    for c in c0.values(): c.wait_send()
    for c in c1.values(): c.wait_send()
    for c in c2.values(): c.wait_send()
    for c in c3.values(): c.wait_send()
    if with_halo:
        halo_wait(x_ref, xg, xcorner, 8)
        halo_wait(vg.at[1], vg, vcorner, 0)


def run_exchange(kern, coords, cuts, pieces, with_halo=True):
    n = len(pieces)
    vm = pl.BlockSpec(memory_space=pltpu.VMEM)
    dma = pltpu.SemaphoreType.DMA
    return pl.pallas_call(
        functools.partial(exchange, pieces, with_halo, cuts),
        out_shape=[jax.ShapeDtypeStruct((3, 3, 128, 128), f32)] * 2 + [jax.ShapeDtypeStruct((3, 2, 3, 8, 128), f32)] * 2,
        in_specs=[pl.BlockSpec(memory_space=pl.ANY), vm],
        out_specs=[vm] * 4,
        scratch_shapes=[
            pltpu.VMEM((3, 2, 4, 128, 128), f32), pltpu.VMEM((3, 2, 4, 128, 128), f32),
            pltpu.VMEM((2, 3, 2, 64, 128), f32), pltpu.VMEM((2, 3, 2, 128, 128), f32),
            pltpu.VMEM((3, 128, 128), f32),
            dma((n,)), dma((4 * n,)), dma((4 * n,)), dma((2 * n,)), dma((2 * n,)), dma((2 * n,)), dma((2 * n,)),
            dma((n,)), dma((n,)), dma((16,)), dma((16,))],
        compiler_params=pltpu.CompilerParams(collective_id=0, has_side_effects=True, vmem_limit_bytes=40 * 2**20),
        name="event_sum_and_halo",
    )(kern, coords)
C2 = 1.4426950408889634 / 0.72
CLASSES = (9, 8, 7, 6, 5, 4)
ZERO = 391
LIMIT = 1.5
SHIFT = C2 * 3.0 * LIMIT * LIMIT
NT = (((1,), (1,)), ((), ()))
bf16 = jnp.bfloat16


def plan_slots(ids):
    tiles = ids.shape[0]
    valid = ids >= 0
    safe = jnp.maximum(ids, 0)
    row, col = safe // 130, safe % 130
    spot = jnp.where(col == 0, 384 + 2 * row, jnp.where(col == 129, 385 + 2 * row, row * 128 + col - 1))
    rank = jnp.cumsum(valid, axis=1) - 1
    j = jnp.arange(9)
    hit = (rank[:, None, :] == j[None, :, None]) & valid[:, None, :]
    named = jnp.sum(jnp.where(hit, spot[:, None, :], 0), axis=2) + jnp.where(jnp.any(hit, axis=2), 0, ZERO)
    named = jnp.concatenate([named, jnp.full((8, 9), ZERO)], axis=0)
    size = jnp.maximum(jnp.sum(valid, axis=1), CLASSES[-1])
    member = size[:, None] == jnp.array(CLASSES)[None, :]
    counts = jnp.sum(member, axis=0)
    pairs = (counts + 1) // 2
    start = 2 * (jnp.cumsum(pairs) - pairs)
    within = jnp.cumsum(member, axis=0) - 1
    place = jnp.sum(jnp.where(member, start[None, :] + within, 0), axis=1)
    slots = jnp.arange(144)
    found = place[None, :] == slots[:, None]
    order = jnp.sum(jnp.where(found, jnp.arange(tiles)[None, :], 0), axis=1) + jnp.where(jnp.any(found, axis=1), 0, tiles)
    i32 = jnp.int32
    return order.astype(i32), jnp.concatenate([start, pairs]).astype(i32), named.reshape(-1).astype(i32)


def smooth_kernel(order, spans, named, vg, xg, vc, xc, out, lp, vtab, xtab, ctab, sm, ha, hb, pa, pb, ra, rb):
    vtab[...] = jnp.zeros_like(vtab)
    row8 = lax.broadcasted_iota(jnp.int32, (1, 8, 128), 1)

    def three(a, b, c):
        n = a.shape[0]
        wide = lambda r: jnp.broadcast_to(r[:, None, :], (n, 8, 128))
        return jnp.where(row8 == 0, wide(a), jnp.where(row8 == 1, wide(b), wide(c)))

    def values(at, v):
        n = v.shape[0]
        v = jnp.where(row8 < 3, v, jnp.where(row8 == 3, 1.0, 0.0))
        hi = v.astype(bf16).astype(f32)
        vtab[at:at + n] = jnp.concatenate([hi, v - hi], axis=1).astype(bf16)

    for s in range(3):
        for g in range(0, 128, 32):
            at = s * 128 + g
            xtab[at:at + 32] = three(*[xg[s, k, g:g + 32] for k in range(3)])
            values(at, three(*[vg[s, k, g:g + 32] for k in range(3)]))
        for e, r in ((0, 7), (1, 0)):
            at = 384 + 2 * s + e
            xtab[at:at + 1] = three(*[xc[s, e, k, r:r + 1] for k in range(3)])
            values(at, three(*[vc[s, e, k, r:r + 1] for k in range(3)]))
    xtab[390:] = jnp.zeros((10, 8, 128), f32)
    own = xg[1]
    low, high = jnp.min(own, axis=2, keepdims=True), jnp.max(own, axis=2, keepdims=True)
    reach = jnp.max(0.5 * high - 0.5 * low)
    mid = jnp.broadcast_to(0.5 * high + 0.5 * low, own.shape)
    for g in range(0, 128, 32):
        ctab[g:g + 32] = three(*[mid[k, g:g + 32] for k in range(3)])
    ctab[128:] = jnp.zeros((8, 8, 128), f32)

    def columns(rows, px):
        for a in range(3):
            px[a] = jnp.transpose(jnp.broadcast_to(rows[a:a + 1], (128, 128)))

    def prepare(n, t, px, rows):
        c = ctab[t]
        columns(xtab[128 + t] - c, px)
        for s in range(n):
            y = jnp.clip(xtab[named[t * 9 + s]] - c, -1e4, 1e4)
            b = y * y
            rows[s] = y * (2 * C2)
            rows[s, 3:4] = (b[0:1] + b[1:2] + b[2:3]) * (-C2) - SHIFT

    def weigh(n, px, rows, h):
        for p in range(0, 128, 32):
            cols = [px[a, p:p + 32] for a in range(3)]
            for s in range(n):
                r = [jnp.broadcast_to(rows[s, k:k + 1], (32, 128)) for k in range(4)]
                w = jnp.exp2(((cols[0] * r[0] + r[3]) + cols[1] * r[1]) + cols[2] * r[2])
                hi = w.astype(bf16)
                h[p:p + 32, s * 128:(s + 1) * 128] = hi
                h[128 + p:160 + p, s * 128:(s + 1) * 128] = (w - hi.astype(f32)).astype(bf16)

    def settle(t, r):
        total = r[:, :128] + r[:, 128:]
        mean = (total[0:3] + total[8:11]) / total[3:4]
        for k in range(3):
            sm[k, pl.ds(t, 1)] = mean[k:k + 1]

    def gather(n, t, h):
        v = jnp.concatenate([vtab[named[t * 9 + s]] for s in range(n)], axis=1)
        settle(t, lax.dot_general(v, h[:, :n * 128], NT, preferred_element_type=f32))

    @pl.when(reach <= LIMIT)
    def _():
        for c, n in enumerate(CLASSES):
            first, pairs = spans[c], spans[len(CLASSES) + c]

            @pl.when(pairs > 0)
            def _(n=n, first=first, pairs=pairs):
                prepare(n, order[first], pa, ra)

                def body(i, _):
                    at = first + 2 * i
                    t, u, nxt = order[at], order[at + 1], order[at + 2]
                    before = jnp.where(i == 0, 128, order[jnp.maximum(at - 1, 0)])
                    prepare(n, u, pb, rb)
                    gather(n, before, hb)
                    weigh(n, pa, ra, ha)
                    prepare(n, nxt, pa, ra)
                    gather(n, t, ha)
                    weigh(n, pb, rb, hb)
                    return 0

                lax.fori_loop(0, pairs, body, 0)
                gather(n, order[first + 2 * pairs - 1], hb)

    @pl.when(jnp.logical_not(reach <= LIMIT))
    def _():
        def tile(t, _):
            columns(xtab[128 + t], pa)

            def slot(s, total):
                g = named[t * 9 + s]
                q = xtab[g]
                dist = jnp.zeros((128, 128), f32)
                for a in range(3):
                    diff = pa[a] - q[a:a + 1]
                    dist = dist + diff * diff
                w = jnp.exp(dist * (-1.0 / 0.72))
                hi = w.astype(bf16)
                both = jnp.concatenate([hi, (w - hi.astype(f32)).astype(bf16)], axis=0)
                return total + lax.dot_general(vtab[g], both, NT, preferred_element_type=f32)

            settle(t, lax.fori_loop(0, 9, slot, jnp.zeros((16, 256), f32)))
            return 0

        lax.fori_loop(0, 128, tile, 0)

    got = sm[:, 0:128]
    out[...] = got
    spread = jnp.sqrt(got * got + 0.01)
    lp[...] = jnp.sum(spread.reshape(48, 8, 128), axis=0)


def run_smooth(order, spans, named, vg, xg, vc, xc):
    vm, sm = pl.BlockSpec(memory_space=pltpu.VMEM), pl.BlockSpec(memory_space=pltpu.SMEM)
    return pl.pallas_call(
        smooth_kernel,
        out_shape=[jax.ShapeDtypeStruct((3, 128, 128), f32), jax.ShapeDtypeStruct((8, 128), f32)],
        in_specs=[sm] * 3 + [vm] * 4,
        out_specs=[vm] * 2,
        scratch_shapes=[
            pltpu.VMEM((400, 16, 128), bf16), pltpu.VMEM((400, 8, 128), f32), pltpu.VMEM((136, 8, 128), f32),
            pltpu.VMEM((3, 136, 128), f32),
            pltpu.VMEM((256, 1152), bf16), pltpu.VMEM((256, 1152), bf16),
            pltpu.VMEM((3, 128, 128), f32), pltpu.VMEM((3, 128, 128), f32),
            pltpu.VMEM((9, 8, 128), f32), pltpu.VMEM((9, 8, 128), f32)],
        compiler_params=pltpu.CompilerParams(vmem_limit_bytes=40 * 2**20),
        name="smooth_tiles",
    )(order, spans, named, vg, xg, vc, xc)


def total_kernel(cuts, part, out, held, ss, rs):
    ev, cut = lax.axis_index("ev"), lax.axis_index("cuts")
    steps = []
    lows = 8 if cuts % 8 == 0 else cuts
    high = cuts // lows
    steps.append([(lax.rem(ev + d, 16), cut) for d in range(1, 16)])
    base, lane = lax.div(cut, lows) * lows, lax.rem(cut, lows)
    steps.append([(ev, base + lax.rem(lane + d, lows)) for d in range(1, lows)])
    if high > 1:
        steps.append([(ev, lax.rem(cut + d * lows, cuts)) for d in range(1, high)])
    barrier = pltpu.get_barrier_semaphore()
    n = 0
    for step in steps:
        for dev in step:
            pl.semaphore_signal(barrier, inc=1, device_id=dev, device_id_type=MESH)
            n += 1
    here = jnp.sum(part[...], axis=(0, 1), keepdims=True)
    held[0] = jnp.broadcast_to(here, (8, 128))
    pl.semaphore_wait(barrier, n)
    slot, mine, sem = 1, 0, 0
    for step in steps:
        copies = []
        for d, dev in enumerate(step):
            c = pltpu.make_async_remote_copy(src_ref=held.at[mine], dst_ref=held.at[slot + d], send_sem=ss.at[sem], recv_sem=rs.at[sem],
                                             device_id=dev, device_id_type=MESH)
            c.start()
            copies.append(c)
            sem += 1
        total = held[mine]
        for d, c in enumerate(copies):
            c.wait_recv()
            total = total + held[slot + d]
        for c in copies:
            c.wait_send()
        slot += len(step)
        mine = slot
        held[mine] = total
        slot += 1
    out[...] = held[mine]


def run_total(part, cuts):
    vm = pl.BlockSpec(memory_space=pltpu.VMEM)
    dma = pltpu.SemaphoreType.DMA
    return pl.pallas_call(
        functools.partial(total_kernel, cuts),
        out_shape=jax.ShapeDtypeStruct((8, 128), f32),
        in_specs=[vm], out_specs=vm,
        scratch_shapes=[pltpu.VMEM((64, 8, 128), f32), dma((48,)), dma((48,))],
        compiler_params=pltpu.CompilerParams(collective_id=1, has_side_effects=True),
        name="sum_over_devices",
    )(part)


def on_device(cuts, kernels, coords, neighbours):
    pieces = [(0, 64), (64, 128)]
    plan = plan_slots(neighbours[0])
    vg, xg, vc, xc = run_exchange(kernels.reshape(3, 2, 4, 2, 128, 128), coords.reshape(3, 128, 128), cuts, pieces)
    smoothed, part = run_smooth(*plan, vg, xg, vc, xc)
    total = run_total(part, cuts)[0, 0]
    smoothed = smoothed.reshape(3, 1, 16384)
    everything = 3 * 16384 * 16 * cuts
    return smoothed, total / everything / jnp.sqrt(smoothed * smoothed + 0.01)


def solution(mesh):
    cuts = mesh.shape["cuts"]
    return jax.shard_map(
        functools.partial(on_device, cuts),
        mesh=mesh,
        in_specs=(P("ev", None, "cuts", None), P(None, "cuts", "ev"), P("cuts", "ev", None)),
        out_specs=(P(None, "cuts", "ev"), P(None, "cuts", "ev")),
        check_vma=False,
    )
```

```python
import functools
import jax
import jax.numpy as jnp
from jax import lax
from jax.experimental import pallas as pl
from jax.experimental.pallas import tpu as pltpu
from jax.sharding import PartitionSpec as P

MESH = pl.DeviceIdType.MESH
f32 = jnp.float32
bf16 = jnp.bfloat16
C2 = 1.4426950408889634 / 0.72
CLASSES = (9, 8, 7, 6, 5)
PLACES = 144
ZERO = 391
LIMIT = 1.5
SHIFT = C2 * 3.0 * LIMIT * LIMIT
NT = (((1,), (1,)), ((), ()))
VM1, VM2 = 16, 12
PIECES = ((0, 48, True), (48, 96, True), (96, 128, False))


def three(a, b, c):
    n = a.shape[0]
    row = lax.broadcasted_iota(jnp.int32, (1, 8, 128), 1)
    wide = lambda r: jnp.broadcast_to(r[:, None, :], (n, 8, 128))
    return jnp.where(row == 0, wide(a), jnp.where(row == 1, wide(b), wide(c)))


def plan_slots(nb, plan, named, reach):
    i32 = jnp.int32
    zero = jnp.zeros((1, 128), i32)
    count = zero
    found = [zero + ZERO for _ in range(9)]
    for s in range(9):
        v = nb[s:s + 1]
        row = jnp.where(v >= 260, 2, jnp.where(v >= 130, 1, 0))
        col = v - 130 * row
        spot = jnp.where(col == 0, 384 + 2 * row, jnp.where(col == 129, 385 + 2 * row, row * 128 + col - 1))
        for j in range(s + 1):
            found[j] = jnp.where((v >= 0) & (count == j), spot, found[j])
        count = count + jnp.where(v >= 0, 1, 0)
    named[...] = jnp.concatenate(found + [zero] * 7, axis=0)
    size = jnp.maximum(count, CLASSES[-1])
    member = jnp.concatenate([jnp.where(size == n, 1.0, 0.0) for n in CLASSES] + [jnp.zeros((3, 128), f32)], axis=0)
    upto = lax.broadcasted_iota(i32, (128, 128), 0) <= lax.broadcasted_iota(i32, (128, 128), 1)
    run = jnp.dot(member.astype(bf16), jnp.where(upto, 1.0, 0.0).astype(bf16), preferred_element_type=f32)
    lane = lax.broadcasted_iota(i32, (1, 256), 1)
    start = jnp.zeros((1, 1), f32)
    place = jnp.zeros((1, 128), f32)
    spans = jnp.where(lane == 12, jnp.where(reach <= LIMIT, 1.0, 0.0), 0.0)
    for c in range(len(CLASSES)):
        fours = jnp.floor((jnp.sum(member[c:c + 1], axis=1, keepdims=True) + 3.0) * 0.25)
        place = place + member[c:c + 1] * (start + run[c:c + 1] - 1.0)
        spans = spans + jnp.where(lane == c, start, 0.0) + jnp.where(lane == len(CLASSES) + c, fours, 0.0)
        start = start + 4.0 * fours
    hit = jnp.where(place.astype(i32) == lax.broadcasted_iota(i32, (256, 128), 0), 1.0, 0.0).astype(bf16)
    tile = lax.broadcasted_iota(i32, (8, 128), 1)
    what = jnp.where(lax.broadcasted_iota(i32, (8, 128), 0) == 0, tile - 128, 0).astype(f32).astype(bf16)
    order = lax.dot_general(what, hit, NT, preferred_element_type=f32)[0:1] + 128.0
    plan[...] = jnp.concatenate([order, spans, jnp.zeros((6, 256), f32)], axis=0).astype(i32)


def exchange(cuts, d, x_ref, nb, vg, vc, xg, xc, cols0, cols1, cols2, feats, plan, named,
             mine, other, x1, x2, yb, ybig, xtab, ctab, yown, named_s, plan_s, tmp_sem,
             loc_sem, s0, r0, s1, r1, s2, r2, s3, r3, sh, rh):
    ev = lax.axis_index("ev")
    cut = lax.axis_index("cuts")
    core = lax.rem(ev, 2)
    x = lax.rem(lax.div(ev, 2), 4)
    yh = lax.div(ev, 8)
    yl = lax.rem(cut, 2)

    def at(y_, x_, c_):
        return (y_ * 8 + x_ * 2 + c_, cut)

    xp, xm, xo = lax.rem(x + 1, 4), lax.rem(x + 3, 4), lax.rem(x + 2, 4)
    twin = at(yh, x, 1 - core)
    right, left = at(yh, xp, core), at(yh, xm, core)
    across = at(1 - yh, x, core)
    beside = (ev, cut + 1 - 2 * yl)
    ahead, behind = cut + 2 - 4 * yl, cut - 2 + 4 * yl
    ok_ahead = (ahead >= 0) & (ahead < cuts)
    ok_behind = (behind >= 0) & (behind < cuts)
    near, far = 2 - 2 * yl, 2 * yl
    rel = [(de, dc) for de in (-1, 1) for dc in (-1, 0, 1)]

    def exists(de, dc):
        ok = (ev + de >= 0) & (ev + de < 16)
        if dc:
            ok = ok & (cut + dc >= 0) & (cut + dc < cuts)
        return ok

    barrier = pltpu.get_barrier_semaphore()
    for dev in (twin, right, left, across, beside):
        pl.semaphore_signal(barrier, inc=1, device_id=dev, device_id_type=MESH)
    expect = 5
    for ok, c in ((ok_ahead, ahead), (ok_behind, behind)):
        @pl.when(ok)
        def _(c=c):
            pl.semaphore_signal(barrier, inc=1, device_id=(ev, c), device_id_type=MESH)
        expect = expect + ok.astype(jnp.int32)
    for de, dc in rel:
        @pl.when(exists(de, dc))
        def _(de=de, dc=dc):
            pl.semaphore_signal(barrier, inc=1, device_id=(ev + de, cut + dc), device_id_type=MESH)
        expect = expect + exists(de, dc).astype(jnp.int32)

    n = len(PIECES)
    rows = [pl.ds(a, b - a) for a, b, _ in PIECES]
    ha = [pl.ds(a, (b - a) // 2) for a, b, _ in PIECES]
    hb = [pl.ds(a + (b - a) // 2, (b - a) // 2) for a, b, _ in PIECES]
    hx = [pl.ds(a // 2, (b - a) // 2) for a, b, _ in PIECES]

    locs = []
    for p in range(n):
        c = pltpu.make_async_copy(d.at[:, :, :, core, rows[p]], mine.at[:, :, :, rows[p]], loc_sem.at[p])
        c.start()
        locs.append(c)
    pl.semaphore_wait(barrier, expect)

    def remote(src, dst, ss, rs, dev, start=True):
        c = pltpu.make_async_remote_copy(src_ref=src, dst_ref=dst, send_sem=ss, recv_sem=rs,
                                         device_id=dev, device_id_type=MESH)
        if start:
            c.start()
        return c

    order = [xo, xp, xm, x]
    c0 = {}
    for p in range(n):
        for i, xx in enumerate(order):
            c0[p, i] = remote(d.at[:, :, xx, 1 - core, rows[p]], other.at[:, :, xx, rows[p]],
                              s0.at[p * 4 + i], r0.at[p * 4 + i], twin)

    def lend(full, part, sem):
        return remote(full.at[1, :, part], full.at[far, :, part], sh.at[sem], rh.at[sem], beside, False)

    def pass_on(full, part, sem):
        return remote(full.at[near, :, part], full.at[far, :, part], sh.at[sem], rh.at[sem], (ev, ahead), False)

    def corners(full, small, base, act):
        for i, (de, dc) in enumerate(rel):
            c = remote(full.at[1, :, pl.ds(120 if de > 0 else 0, 8)], small.at[1 - dc, 0 if de > 0 else 1],
                       sh.at[base + i], rh.at[base + i], (ev + de, cut + dc), False)
            if act == "start":
                pl.when(exists(de, dc))(c.start)
            elif act == "send":
                pl.when(exists(de, dc))(c.wait_send)
            else:
                pl.when(exists(-de, -dc))(c.wait_recv)

    whole = pl.ds(0, 128)
    xg[1] = x_ref[...]
    lend(xg, whole, 12).start()
    corners(xg, xc, 6, "start")

    own = x_ref[...]
    low, high = jnp.min(own, axis=2, keepdims=True), jnp.max(own, axis=2, keepdims=True)
    mid = jnp.broadcast_to(0.5 * high + 0.5 * low, own.shape)
    yown[...] = own - mid
    for g in range(0, 128, 32):
        ctab[g:g + 32] = three(*[mid[k, g:g + 32] for k in range(3)])
        xtab[128 + g:160 + g] = three(*[own[k, g:g + 32] for k in range(3)])
    xtab[390:] = jnp.zeros((10, 8, 128), f32)
    plan_slots(nb[...], plan, named, jnp.max(0.5 * high - 0.5 * low, axis=(0, 1), keepdims=True)[0])
    local = [pltpu.make_async_copy(named, named_s, tmp_sem.at[0]), pltpu.make_async_copy(plan, plan_s, tmp_sem.at[1])]
    for c in local:
        c.start()
    for c in local:
        c.wait()

    def columns(j, _):
        t = jnp.clip(plan_s[0, j], 0, 127)
        for k, c in enumerate((cols0, cols1, cols2)):
            c[j] = jnp.transpose(jnp.broadcast_to(yown[k, pl.ds(t, 1)], (128, 128)))
        return 0

    def features(j, _):
        t = jnp.clip(plan_s[0, j], 0, 127)
        c = ctab[t]
        for s in range(9):
            y = jnp.clip(xtab[jnp.clip(named_s[s, t], 0, 399)] - c, -1e4, 1e4)
            b = y * y
            feats[j * 9 + s] = y * (2 * C2)
            feats[j * 9 + s, 3:4] = (b[0:1] + b[1:2] + b[2:3]) * (-C2) - SHIFT
        return 0

    def some_columns(i):
        lax.fori_loop(18 * i, 18 * i + 18, columns, 0)

    def neighbour_positions():
        pl.when(ok_behind)(pass_on(xg, whole, 13).wait_recv)
        corners(xg, xc, 6, "recv")
        for s in (0, 2):
            for g in range(0, 128, 32):
                xtab[s * 128 + g:s * 128 + g + 32] = three(*[xg[s, k, g:g + 32] for k in range(3)])
        for s in range(3):
            for e, r in ((0, 7), (1, 0)):
                xtab[384 + 2 * s + e:385 + 2 * s + e] = three(*[xc[s, e, k, r:r + 1] for k in range(3)])

    c1, c2, c3 = {}, {}, {}

    def arrive(p, xx, i):
        c0[p, i].wait_recv()
        mine[:, :, xx, rows[p]] += other[:, :, xx, rows[p]]

    def level(p, k):
        first = PIECES[p][2]
        if first:
            ys, step = slice(None), k
        else:
            ys, step = pl.ds(yh, 1), k - 1
        if k == 1:
            locs[p].wait()
            arrive(p, xo, 0)
            if not first:
                for i in (1, 2, 3):
                    arrive(p, order[i], i)
                c3[p] = remote(mine.at[:, 1 - yh, :, rows[p]], ybig.at[:, :, pl.ds(0, PIECES[p][1] - PIECES[p][0])], s3.at[p], r3.at[p], across)
        if k == 2 and not first:
            c3[p].wait_recv()
            mine[:, yh, :, rows[p]] += ybig[:, :, pl.ds(0, PIECES[p][1] - PIECES[p][0])]
        if step == 1:
            for side, half, dev in ((0, ha[p], right), (1, hb[p], left)):
                c1[p, side] = remote(mine.at[:, ys, xo, half], x1.at[side, :, ys, hx[p]], s1.at[2 * p + side], r1.at[2 * p + side], dev)
        elif step == 2:
            for side, xx, half, dev in ((0, xp, ha[p], right), (1, xm, hb[p], left)):
                if first:
                    arrive(p, xx, 1 + side)
                c1[p, side].wait_recv()
                mine[:, ys, xx, half] += x1[side, :, ys, hx[p]]
                c2[p, side] = remote(mine.at[:, ys, xx, rows[p]], x2.at[side, :, ys, rows[p]], s2.at[2 * p + side], r2.at[2 * p + side], dev)
        elif step == 3:
            if first:
                arrive(p, x, 3)
            for side in (0, 1):
                c2[p, side].wait_recv()
                mine[:, ys, x, rows[p]] += x2[side, :, ys, rows[p]]
            if first:
                c3[p] = remote(mine.at[:, 1 - yh, x, rows[p]], yb.at[:, rows[p]], s3.at[p], r3.at[p], across)
            else:
                vg[1, :, rows[p]] = mine[:, yh, x, rows[p]]
                lend(vg, rows[p], 14 + p).start()
        elif step == 4:
            c3[p].wait_recv()
            vg[1, :, rows[p]] = mine[:, yh, x, rows[p]] + yb[:, rows[p]]
            lend(vg, rows[p], 14 + p).start()

    some_columns(0)
    for p in range(n):
        level(p, 1)
    some_columns(1)
    lend(xg, whole, 12).wait_recv()
    pl.when(ok_ahead)(pass_on(xg, whole, 13).start)
    some_columns(2)
    for p in range(n):
        level(p, 2)
    some_columns(3)
    some_columns(4)
    for p in range(n):
        level(p, 3)
    some_columns(5)
    neighbour_positions()
    lax.fori_loop(0, PLACES // 2, features, 0)
    for p in range(n):
        level(p, 4)
    corners(vg, vc, 0, "start")
    lax.fori_loop(PLACES // 2, PLACES, features, 0)
    some_columns(6)
    for p in reversed(range(n)):
        lend(vg, rows[p], 14 + p).wait_recv()
        pl.when(ok_ahead)(pass_on(vg, rows[p], 14 + n + p).start)
    some_columns(7)
    for p in range(n):
        pl.when(ok_behind)(pass_on(vg, rows[p], 14 + n + p).wait_recv)
    corners(vg, vc, 0, "recv")

    for c in list(c0.values()) + list(c1.values()) + list(c2.values()) + list(c3.values()):
        c.wait_send()
    lend(xg, whole, 12).wait_send()
    pl.when(ok_ahead)(pass_on(xg, whole, 13).wait_send)
    for p in range(n):
        lend(vg, rows[p], 14 + p).wait_send()
        pl.when(ok_ahead)(pass_on(vg, rows[p], 14 + n + p).wait_send)
    corners(xg, xc, 6, "send")
    corners(vg, vc, 0, "send")


def run_exchange(kern, coords, nb, cuts):
    n = len(PIECES)
    deep = max(b - a for a, b, first in PIECES if not first)
    vm = pl.BlockSpec(memory_space=pltpu.VMEM)
    dma = pltpu.SemaphoreType.DMA
    shape = jax.ShapeDtypeStruct
    return pl.pallas_call(
        functools.partial(exchange, cuts),
        out_shape=[shape((3, 3, 128, 128), f32), shape((3, 2, 3, 8, 128), f32),
                   shape((3, 3, 128, 128), f32), shape((3, 2, 3, 8, 128), f32),
                   *[shape((PLACES, 128, 128), f32)] * 3, shape((PLACES * 9, 8, 128), f32),
                   shape((8, 256), jnp.int32), shape((16, 128), jnp.int32)],
        in_specs=[pl.BlockSpec(memory_space=pltpu.HBM), vm, vm],
        out_specs=[vm] * 10,
        scratch_shapes=[
            pltpu.VMEM((3, 2, 4, 128, 128), f32), pltpu.VMEM((3, 2, 4, 128, 128), f32),
            pltpu.VMEM((2, 3, 2, 64, 128), f32), pltpu.VMEM((2, 3, 2, 128, 128), f32),
            pltpu.VMEM((3, 128, 128), f32), pltpu.VMEM((3, 4, deep, 128), f32),
            pltpu.VMEM((400, 8, 128), f32), pltpu.VMEM((128, 8, 128), f32), pltpu.VMEM((3, 128, 128), f32),
            pltpu.SMEM((16, 128), jnp.int32), pltpu.SMEM((8, 256), jnp.int32), dma((2,)),
            dma((n,)), dma((4 * n,)), dma((4 * n,)), dma((2 * n,)), dma((2 * n,)), dma((2 * n,)), dma((2 * n,)),
            dma((n,)), dma((n,)), dma((14 + 2 * n,)), dma((14 + 2 * n,))],
        compiler_params=pltpu.CompilerParams(collective_id=0, has_side_effects=True, vmem_limit_bytes=VM1 * 2**20),
        name="event_sum_and_halo",
    )(kern, coords, nb)


def smooth_kernel(plan, named, vg, vc, xg, xc, cols0, cols1, cols2, feats, out, lp, vtab, sm, xtab, pa):
    row8 = lax.broadcasted_iota(jnp.int32, (1, 8, 128), 1)

    def values(at, v):
        n = v.shape[0]
        v = jnp.where(row8 < 3, v, jnp.where(row8 == 3, 1.0, 0.0))
        hi = v.astype(bf16).astype(f32)
        vtab[at:at + n] = jnp.concatenate([hi, v - hi], axis=1).astype(bf16)

    for s in range(3):
        for g in range(0, 128, 32):
            values(s * 128 + g, three(*[vg[s, k, g:g + 32] for k in range(3)]))
        for e, r in ((0, 7), (1, 0)):
            values(384 + 2 * s + e, three(*[vc[s, e, k, r:r + 1] for k in range(3)]))
    vtab[390:] = jnp.zeros((10, 16, 128), bf16)

    def settle(t, r):
        total = r[:, :128] + r[:, 128:]
        mean = (total[0:3] + total[8:11]) / total[3:4]
        for k in range(3):
            sm[k, pl.ds(t, 1)] = mean[k:k + 1]

    def gather(n, t, j):
        tt = jnp.minimum(t, 127)
        col = [c[j] for c in (cols0, cols1, cols2)]
        total = None
        for a in range(0, n, 2):
            both, v = [], []
            for s in range(a, min(a + 2, n)):
                r = [jnp.broadcast_to(feats[j * 9 + s, k:k + 1], (128, 128)) for k in range(4)]
                w = jnp.exp2(((col[0] * r[0] + r[3]) + col[1] * r[1]) + col[2] * r[2])
                hi = w.astype(bf16)
                both.append(jnp.concatenate([hi, (w - hi.astype(f32)).astype(bf16)], axis=0))
                v.append(vtab[named[s, tt]])
            r = lax.dot_general(jnp.concatenate(v, axis=1), jnp.concatenate(both, axis=1), NT, preferred_element_type=f32)
            total = r if total is None else total + r
        return total

    wide = plan[1, 12] == 0

    @pl.when(jnp.logical_not(wide))
    def _():
        for c, n in enumerate(CLASSES):
            first = plan[1, c]

            def body(i, _, n=n, first=first):
                at = first + 4 * i
                t = [plan[0, at + k] for k in range(4)]
                got = [gather(n, t[k], at + k) for k in range(4)]
                for k in range(4):
                    settle(t[k], got[k])
                return 0

            lax.fori_loop(0, plan[1, len(CLASSES) + c], body, 0)

    @pl.when(wide)
    def _():
        for s in range(3):
            for g in range(0, 128, 32):
                xtab[s * 128 + g:s * 128 + g + 32] = three(*[xg[s, k, g:g + 32] for k in range(3)])
            for e, r in ((0, 7), (1, 0)):
                xtab[384 + 2 * s + e:385 + 2 * s + e] = three(*[xc[s, e, k, r:r + 1] for k in range(3)])
        xtab[390:] = jnp.zeros((10, 8, 128), f32)

        def tile(t, _):
            here = xtab[128 + t]
            for a in range(3):
                pa[a] = jnp.transpose(jnp.broadcast_to(here[a:a + 1], (128, 128)))

            def slot(s, total):
                g = named[s, t]
                q = xtab[g]
                dist = jnp.zeros((128, 128), f32)
                for a in range(3):
                    diff = pa[a] - q[a:a + 1]
                    dist = dist + diff * diff
                w = jnp.exp(dist * (-1.0 / 0.72))
                hi = w.astype(bf16)
                both = jnp.concatenate([hi, (w - hi.astype(f32)).astype(bf16)], axis=0)
                return total + lax.dot_general(vtab[g], both, NT, preferred_element_type=f32)

            settle(t, lax.fori_loop(0, 9, slot, jnp.zeros((16, 256), f32)))
            return 0

        lax.fori_loop(0, 128, tile, 0)

    got = sm[:, 0:128]
    out[...] = got
    lp[...] = jnp.sum(jnp.sqrt(got * got + 0.01).reshape(48, 8, 128), axis=0)


def run_smooth(vg, vc, xg, xc, cols0, cols1, cols2, feats, plan, named):
    vm, sm = pl.BlockSpec(memory_space=pltpu.VMEM), pl.BlockSpec(memory_space=pltpu.SMEM)
    return pl.pallas_call(
        smooth_kernel,
        out_shape=[jax.ShapeDtypeStruct((3, 128, 128), f32), jax.ShapeDtypeStruct((8, 128), f32)],
        in_specs=[sm] * 2 + [vm] * 8,
        out_specs=[vm] * 2,
        scratch_shapes=[
            pltpu.VMEM((400, 16, 128), bf16), pltpu.VMEM((3, 136, 128), f32),
            pltpu.VMEM((400, 8, 128), f32), pltpu.VMEM((3, 128, 128), f32)],
        compiler_params=pltpu.CompilerParams(vmem_limit_bytes=VM2 * 2**20),
        name="smooth_tiles",
    )(plan, named, vg, vc, xg, xc, cols0, cols1, cols2, feats)


def total_kernel(cuts, smoothed, part, out, held, ss, rs):
    ev, cut = lax.axis_index("ev"), lax.axis_index("cuts")
    yh, inner = lax.div(ev, 8) * 8, lax.rem(ev, 8)
    steps = [[(yh + lax.rem(inner + d, 8), cut) for d in range(1, 8)]]
    low = min(4, cuts)
    base, lane = lax.div(cut, low) * low, lax.rem(cut, low)
    steps.append([(lax.rem(ev + 8 * a, 16), base + lax.rem(lane + b, low)) for a in (0, 1) for b in range(low) if a + b])
    if cuts > low:
        steps.append([(ev, lax.rem(cut + d * low, cuts)) for d in range(1, cuts // low)])
    barrier = pltpu.get_barrier_semaphore()
    n = 0
    for step in steps:
        for dev in step:
            pl.semaphore_signal(barrier, inc=1, device_id=dev, device_id_type=MESH)
            n += 1
    held[0] = jnp.broadcast_to(jnp.sum(part[...], axis=(0, 1), keepdims=True), (1, 128))
    pl.semaphore_wait(barrier, n)
    got = smoothed[...]
    spread = jnp.sqrt(got * got + 0.01)
    slot, mine, copies = 1, 0, []
    for k, step in enumerate(steps):
        m = len(step)
        for d, dev in enumerate(step):
            c = pltpu.make_async_remote_copy(src_ref=held.at[mine], dst_ref=held.at[slot + d],
                                             send_sem=ss.at[slot + d], recv_sem=rs.at[slot + d], device_id=dev, device_id_type=MESH)
            c.start()
            copies.append(c)
        total = held[mine]
        for d in range(m):
            copies[-m + d].wait_recv()
        for d in range(m):
            total = total + held[slot + d]
        slot += m
        mine = slot
        held[mine] = total
        slot += 1
    everything = 3 * 16384 * 16 * cuts
    out[...] = held[mine, 0:1, 0:1] / everything / spread
    for c in copies:
        c.wait_send()


def run_total(smoothed, part, cuts):
    vm = pl.BlockSpec(memory_space=pltpu.VMEM)
    dma = pltpu.SemaphoreType.DMA
    return pl.pallas_call(
        functools.partial(total_kernel, cuts),
        out_shape=jax.ShapeDtypeStruct((3, 128, 128), f32),
        in_specs=[vm, vm], out_specs=vm,
        scratch_shapes=[pltpu.VMEM((32, 1, 128), f32), dma((32,)), dma((32,))],
        compiler_params=pltpu.CompilerParams(collective_id=1, has_side_effects=True, vmem_limit_bytes=8 * 2**20),
        name="sum_over_devices",
    )(smoothed, part)


def on_device(cuts, kernels, coords, neighbours):
    got = run_exchange(kernels.reshape(3, 2, 4, 2, 128, 128), coords.reshape(3, 128, 128), neighbours[0].T, cuts)
    smoothed, part = run_smooth(*got)
    weights = run_total(smoothed, part, cuts)
    return smoothed.reshape(3, 1, 16384), weights.reshape(3, 1, 16384)


def solution(mesh):
    cuts = mesh.shape["cuts"]
    return jax.shard_map(
        functools.partial(on_device, cuts),
        mesh=mesh,
        in_specs=(P("ev", None, "cuts", None), P(None, "cuts", "ev"), P("cuts", "ev", None)),
        out_specs=(P(None, "cuts", "ev"), P(None, "cuts", "ev")),
        check_vma=False,
    )
```

```python
import functools
import jax
import jax.numpy as jnp
from jax import lax
from jax.experimental import pallas as pl
from jax.experimental.pallas import tpu as pltpu
from jax.sharding import PartitionSpec as P

MESH = pl.DeviceIdType.MESH
f32 = jnp.float32
bf16 = jnp.bfloat16
C2 = 1.4426950408889634 / 0.72
CLASSES = (9, 8, 7, 6, 5)
PLACES = 144
ZERO = 391
LIMIT = 1.5
SHIFT = C2 * 3.0 * LIMIT * LIMIT
NT = (((1,), (1,)), ((), ()))
VM1, VM2 = 16, 12
PIECES = ((0, 48, True), (48, 96, True), (96, 128, False))


def three(a, b, c):
    n = a.shape[0]
    row = lax.broadcasted_iota(jnp.int32, (1, 8, 128), 1)
    wide = lambda r: jnp.broadcast_to(r[:, None, :], (n, 8, 128))
    return jnp.where(row == 0, wide(a), jnp.where(row == 1, wide(b), wide(c)))


def plan_slots(nb, plan, named, reach):
    i32 = jnp.int32
    zero = jnp.zeros((1, 128), i32)
    count = zero
    found = [zero + ZERO for _ in range(9)]
    for s in range(9):
        v = nb[s:s + 1]
        row = jnp.where(v >= 260, 2, jnp.where(v >= 130, 1, 0))
        col = v - 130 * row
        spot = jnp.where(col == 0, 384 + 2 * row, jnp.where(col == 129, 385 + 2 * row, row * 128 + col - 1))
        for j in range(s + 1):
            found[j] = jnp.where((v >= 0) & (count == j), spot, found[j])
        count = count + jnp.where(v >= 0, 1, 0)
    named[...] = jnp.concatenate(found + [zero] * 7, axis=0)
    size = jnp.maximum(count, CLASSES[-1])
    member = jnp.concatenate([jnp.where(size == n, 1.0, 0.0) for n in CLASSES] + [jnp.zeros((3, 128), f32)], axis=0)
    upto = lax.broadcasted_iota(i32, (128, 128), 0) <= lax.broadcasted_iota(i32, (128, 128), 1)
    run = jnp.dot(member.astype(bf16), jnp.where(upto, 1.0, 0.0).astype(bf16), preferred_element_type=f32)
    lane = lax.broadcasted_iota(i32, (1, 256), 1)
    start = jnp.zeros((1, 1), f32)
    place = jnp.zeros((1, 128), f32)
    spans = jnp.where(lane == 12, jnp.where(reach <= LIMIT, 1.0, 0.0), 0.0)
    for c in range(len(CLASSES)):
        fours = jnp.floor((jnp.sum(member[c:c + 1], axis=1, keepdims=True) + 3.0) * 0.25)
        place = place + member[c:c + 1] * (start + run[c:c + 1] - 1.0)
        spans = spans + jnp.where(lane == c, start, 0.0) + jnp.where(lane == len(CLASSES) + c, fours, 0.0)
        start = start + 4.0 * fours
    hit = jnp.where(place.astype(i32) == lax.broadcasted_iota(i32, (256, 128), 0), 1.0, 0.0).astype(bf16)
    tile = lax.broadcasted_iota(i32, (8, 128), 1)
    what = jnp.where(lax.broadcasted_iota(i32, (8, 128), 0) == 0, tile - 128, 0).astype(f32).astype(bf16)
    order = lax.dot_general(what, hit, NT, preferred_element_type=f32)[0:1] + 128.0
    plan[...] = jnp.concatenate([order, spans, jnp.zeros((6, 256), f32)], axis=0).astype(i32)


def exchange(cuts, d, x_ref, nb, vg, vc, xg, xc, cols0, cols1, cols2, feats, plan, named,
             mine, other, x1, x2, yb, ybig, xtab, ctab, yown, named_s, plan_s, tmp_sem,
             loc_sem, s0, r0, s1, r1, s2, r2, s3, r3, sh, rh):
    ev = lax.axis_index("ev")
    cut = lax.axis_index("cuts")
    core = lax.rem(ev, 2)
    x = lax.rem(lax.div(ev, 2), 4)
    yh = lax.div(ev, 8)
    yl = lax.rem(cut, 2)

    def at(y_, x_, c_):
        return (y_ * 8 + x_ * 2 + c_, cut)

    xp, xm, xo = lax.rem(x + 1, 4), lax.rem(x + 3, 4), lax.rem(x + 2, 4)
    twin = at(yh, x, 1 - core)
    right, left = at(yh, xp, core), at(yh, xm, core)
    across = at(1 - yh, x, core)
    beside = (ev, cut + 1 - 2 * yl)
    ahead, behind = cut + 2 - 4 * yl, cut - 2 + 4 * yl
    ok_ahead = (ahead >= 0) & (ahead < cuts)
    ok_behind = (behind >= 0) & (behind < cuts)
    near, far = 2 - 2 * yl, 2 * yl
    rel = [(de, dc) for de in (-1, 1) for dc in (-1, 0, 1)]

    def exists(de, dc):
        ok = (ev + de >= 0) & (ev + de < 16)
        if dc:
            ok = ok & (cut + dc >= 0) & (cut + dc < cuts)
        return ok

    barrier = pltpu.get_barrier_semaphore()
    for dev in (twin, right, left, across, beside):
        pl.semaphore_signal(barrier, inc=1, device_id=dev, device_id_type=MESH)
    expect = 5
    for ok, c in ((ok_ahead, ahead), (ok_behind, behind)):
        @pl.when(ok)
        def _(c=c):
            pl.semaphore_signal(barrier, inc=1, device_id=(ev, c), device_id_type=MESH)
        expect = expect + ok.astype(jnp.int32)
    for de, dc in rel:
        @pl.when(exists(de, dc))
        def _(de=de, dc=dc):
            pl.semaphore_signal(barrier, inc=1, device_id=(ev + de, cut + dc), device_id_type=MESH)
        expect = expect + exists(de, dc).astype(jnp.int32)

    n = len(PIECES)
    rows = [pl.ds(a, b - a) for a, b, _ in PIECES]
    ha = [pl.ds(a, (b - a) // 2) for a, b, _ in PIECES]
    hb = [pl.ds(a + (b - a) // 2, (b - a) // 2) for a, b, _ in PIECES]
    hx = [pl.ds(a // 2, (b - a) // 2) for a, b, _ in PIECES]

    locs = []
    for p in range(n):
        c = pltpu.make_async_copy(d.at[:, :, :, core, rows[p]], mine.at[:, :, :, rows[p]], loc_sem.at[p])
        c.start()
        locs.append(c)
    pl.semaphore_wait(barrier, expect)

    def remote(src, dst, ss, rs, dev, start=True):
        c = pltpu.make_async_remote_copy(src_ref=src, dst_ref=dst, send_sem=ss, recv_sem=rs,
                                         device_id=dev, device_id_type=MESH)
        if start:
            c.start()
        return c

    order = [xo, xp, xm, x]
    c0 = {}
    for p in range(n):
        for i, xx in enumerate(order):
            c0[p, i] = remote(d.at[:, :, xx, 1 - core, rows[p]], other.at[:, :, xx, rows[p]],
                              s0.at[p * 4 + i], r0.at[p * 4 + i], twin)

    def lend(full, part, sem):
        return remote(full.at[1, :, part], full.at[far, :, part], sh.at[sem], rh.at[sem], beside, False)

    def pass_on(full, part, sem):
        return remote(full.at[near, :, part], full.at[far, :, part], sh.at[sem], rh.at[sem], (ev, ahead), False)

    def corners(full, small, base, act):
        for i, (de, dc) in enumerate(rel):
            c = remote(full.at[1, :, pl.ds(120 if de > 0 else 0, 8)], small.at[1 - dc, 0 if de > 0 else 1],
                       sh.at[base + i], rh.at[base + i], (ev + de, cut + dc), False)
            if act == "start":
                pl.when(exists(de, dc))(c.start)
            elif act == "send":
                pl.when(exists(de, dc))(c.wait_send)
            else:
                pl.when(exists(-de, -dc))(c.wait_recv)

    whole = pl.ds(0, 128)
    xg[1] = x_ref[...]
    lend(xg, whole, 12).start()
    corners(xg, xc, 6, "start")

    own = x_ref[...]
    low, high = jnp.min(own, axis=2, keepdims=True), jnp.max(own, axis=2, keepdims=True)
    mid = jnp.broadcast_to(0.5 * high + 0.5 * low, own.shape)
    yown[...] = own - mid
    for g in range(0, 128, 32):
        ctab[g:g + 32] = three(*[mid[k, g:g + 32] for k in range(3)])
        xtab[128 + g:160 + g] = three(*[own[k, g:g + 32] for k in range(3)])
    xtab[390:] = jnp.zeros((10, 8, 128), f32)
    plan_slots(nb[...], plan, named, jnp.max(0.5 * high - 0.5 * low, axis=(0, 1), keepdims=True)[0])
    local = [pltpu.make_async_copy(named, named_s, tmp_sem.at[0]), pltpu.make_async_copy(plan, plan_s, tmp_sem.at[1])]
    for c in local:
        c.start()
    for c in local:
        c.wait()

    def columns(i, _):
        for j in [6 * i + u for u in range(6)]:
            t = jnp.clip(plan_s[0, j], 0, 127)
            for k, c in enumerate((cols0, cols1, cols2)):
                c[j] = jnp.transpose(jnp.broadcast_to(yown[k, pl.ds(t, 1)], (128, 128)))
        return 0

    def features(i, _):
        for j in [2 * i + u for u in range(2)]:
            t = jnp.clip(plan_s[0, j], 0, 127)
            c = ctab[t]
            made = []
            for s in range(9):
                y = jnp.clip(xtab[jnp.clip(named_s[s, t], 0, 399)] - c, -1e4, 1e4)
                b = y * y
                made.append((y * (2 * C2), (b[0:1] + b[1:2] + b[2:3]) * (-C2) - SHIFT))
            for s, (y, b) in enumerate(made):
                feats[j * 9 + s] = y
                feats[j * 9 + s, 3:4] = b
        return 0

    def some_columns(i):
        lax.fori_loop(3 * i, 3 * i + 3, columns, 0)

    def neighbour_positions():
        pl.when(ok_behind)(pass_on(xg, whole, 13).wait_recv)
        corners(xg, xc, 6, "recv")
        for s in (0, 2):
            for g in range(0, 128, 32):
                xtab[s * 128 + g:s * 128 + g + 32] = three(*[xg[s, k, g:g + 32] for k in range(3)])
        for s in range(3):
            for e, r in ((0, 7), (1, 0)):
                xtab[384 + 2 * s + e:385 + 2 * s + e] = three(*[xc[s, e, k, r:r + 1] for k in range(3)])

    c1, c2, c3 = {}, {}, {}

    def arrive(p, xx, i):
        c0[p, i].wait_recv()
        mine[:, :, xx, rows[p]] += other[:, :, xx, rows[p]]

    def level(p, k):
        first = PIECES[p][2]
        if first:
            ys, step = slice(None), k
        else:
            ys, step = pl.ds(yh, 1), k - 1
        if k == 1:
            locs[p].wait()
            arrive(p, xo, 0)
            if not first:
                for i in (1, 2, 3):
                    arrive(p, order[i], i)
                c3[p] = remote(mine.at[:, 1 - yh, :, rows[p]], ybig.at[:, :, pl.ds(0, PIECES[p][1] - PIECES[p][0])], s3.at[p], r3.at[p], across)
        if k == 2 and not first:
            c3[p].wait_recv()
            mine[:, yh, :, rows[p]] += ybig[:, :, pl.ds(0, PIECES[p][1] - PIECES[p][0])]
        if step == 1:
            for side, half, dev in ((0, ha[p], right), (1, hb[p], left)):
                c1[p, side] = remote(mine.at[:, ys, xo, half], x1.at[side, :, ys, hx[p]], s1.at[2 * p + side], r1.at[2 * p + side], dev)
        elif step == 2:
            for side, xx, half, dev in ((0, xp, ha[p], right), (1, xm, hb[p], left)):
                if first:
                    arrive(p, xx, 1 + side)
                c1[p, side].wait_recv()
                mine[:, ys, xx, half] += x1[side, :, ys, hx[p]]
                c2[p, side] = remote(mine.at[:, ys, xx, rows[p]], x2.at[side, :, ys, rows[p]], s2.at[2 * p + side], r2.at[2 * p + side], dev)
        elif step == 3:
            if first:
                arrive(p, x, 3)
            for side in (0, 1):
                c2[p, side].wait_recv()
                mine[:, ys, x, rows[p]] += x2[side, :, ys, rows[p]]
            if first:
                c3[p] = remote(mine.at[:, 1 - yh, x, rows[p]], yb.at[:, rows[p]], s3.at[p], r3.at[p], across)
            else:
                vg[1, :, rows[p]] = mine[:, yh, x, rows[p]]
                lend(vg, rows[p], 14 + p).start()
        elif step == 4:
            c3[p].wait_recv()
            vg[1, :, rows[p]] = mine[:, yh, x, rows[p]] + yb[:, rows[p]]
            lend(vg, rows[p], 14 + p).start()

    some_columns(0)
    for p in range(n):
        level(p, 1)
    some_columns(1)
    lend(xg, whole, 12).wait_recv()
    pl.when(ok_ahead)(pass_on(xg, whole, 13).start)
    some_columns(2)
    for p in range(n):
        level(p, 2)
    some_columns(3)
    some_columns(4)
    for p in range(n):
        level(p, 3)
    some_columns(5)
    neighbour_positions()
    lax.fori_loop(0, PLACES // 4, features, 0)
    for p in range(n):
        level(p, 4)
    corners(vg, vc, 0, "start")
    lax.fori_loop(PLACES // 4, PLACES // 2, features, 0)
    some_columns(6)
    for p in reversed(range(n)):
        lend(vg, rows[p], 14 + p).wait_recv()
        pl.when(ok_ahead)(pass_on(vg, rows[p], 14 + n + p).start)
    some_columns(7)
    for p in range(n):
        pl.when(ok_behind)(pass_on(vg, rows[p], 14 + n + p).wait_recv)
    corners(vg, vc, 0, "recv")

    for c in list(c0.values()) + list(c1.values()) + list(c2.values()) + list(c3.values()):
        c.wait_send()
    lend(xg, whole, 12).wait_send()
    pl.when(ok_ahead)(pass_on(xg, whole, 13).wait_send)
    for p in range(n):
        lend(vg, rows[p], 14 + p).wait_send()
        pl.when(ok_ahead)(pass_on(vg, rows[p], 14 + n + p).wait_send)
    corners(xg, xc, 6, "send")
    corners(vg, vc, 0, "send")


def run_exchange(kern, coords, nb, cuts):
    n = len(PIECES)
    deep = max(b - a for a, b, first in PIECES if not first)
    vm = pl.BlockSpec(memory_space=pltpu.VMEM)
    dma = pltpu.SemaphoreType.DMA
    shape = jax.ShapeDtypeStruct
    return pl.pallas_call(
        functools.partial(exchange, cuts),
        out_shape=[shape((3, 3, 128, 128), f32), shape((3, 2, 3, 8, 128), f32),
                   shape((3, 3, 128, 128), f32), shape((3, 2, 3, 8, 128), f32),
                   *[shape((PLACES, 128, 128), f32)] * 3, shape((PLACES * 9, 8, 128), f32),
                   shape((8, 256), jnp.int32), shape((16, 128), jnp.int32)],
        in_specs=[pl.BlockSpec(memory_space=pltpu.HBM), vm, vm],
        out_specs=[vm] * 10,
        scratch_shapes=[
            pltpu.VMEM((3, 2, 4, 128, 128), f32), pltpu.VMEM((3, 2, 4, 128, 128), f32),
            pltpu.VMEM((2, 3, 2, 64, 128), f32), pltpu.VMEM((2, 3, 2, 128, 128), f32),
            pltpu.VMEM((3, 128, 128), f32), pltpu.VMEM((3, 4, deep, 128), f32),
            pltpu.VMEM((400, 8, 128), f32), pltpu.VMEM((128, 8, 128), f32), pltpu.VMEM((3, 128, 128), f32),
            pltpu.SMEM((16, 128), jnp.int32), pltpu.SMEM((8, 256), jnp.int32), dma((2,)),
            dma((n,)), dma((4 * n,)), dma((4 * n,)), dma((2 * n,)), dma((2 * n,)), dma((2 * n,)), dma((2 * n,)),
            dma((n,)), dma((n,)), dma((14 + 2 * n,)), dma((14 + 2 * n,))],
        compiler_params=pltpu.CompilerParams(collective_id=0, has_side_effects=True, vmem_limit_bytes=VM1 * 2**20),
        name="event_sum_and_halo",
    )(kern, coords, nb)


def smooth_kernel(plan, named, vg, vc, xg, xc, cols0, cols1, cols2, feats, out, spread, vtab, sm, xtab, pa):
    row8 = lax.broadcasted_iota(jnp.int32, (1, 8, 128), 1)

    def values(at, v):
        n = v.shape[0]
        v = jnp.where(row8 < 3, v, jnp.where(row8 == 3, 1.0, 0.0))
        hi = v.astype(bf16).astype(f32)
        vtab[at:at + n] = jnp.concatenate([hi, v - hi], axis=1).astype(bf16)

    for s in range(3):
        for g in range(0, 128, 32):
            values(s * 128 + g, three(*[vg[s, k, g:g + 32] for k in range(3)]))
        for e, r in ((0, 7), (1, 0)):
            values(384 + 2 * s + e, three(*[vc[s, e, k, r:r + 1] for k in range(3)]))
    vtab[390:] = jnp.zeros((10, 16, 128), bf16)

    def settle(t, r):
        total = r[:, :128] + r[:, 128:]
        mean = (total[0:3] + total[8:11]) / total[3:4]
        for k in range(3):
            sm[k, pl.ds(t, 1)] = mean[k:k + 1]

    def gather(n, t, j):
        tt = jnp.minimum(t, 127)
        col = [c[j] for c in (cols0, cols1, cols2)]
        total = None
        for a in range(0, n, 2):
            both, v = [], []
            for s in range(a, min(a + 2, n)):
                r = [jnp.broadcast_to(feats[j * 9 + s, k:k + 1], (128, 128)) for k in range(4)]
                w = jnp.exp2(((col[0] * r[0] + r[3]) + col[1] * r[1]) + col[2] * r[2])
                hi = w.astype(bf16)
                both.append(jnp.concatenate([hi, (w - hi.astype(f32)).astype(bf16)], axis=0))
                v.append(vtab[named[s, tt]])
            r = lax.dot_general(jnp.concatenate(v, axis=1), jnp.concatenate(both, axis=1), NT, preferred_element_type=f32)
            total = r if total is None else total + r
        return total

    wide = plan[1, 12] == 0

    @pl.when(jnp.logical_not(wide))
    def _():
        for c, n in enumerate(CLASSES):
            first = plan[1, c]

            def body(i, _, n=n, first=first):
                at = first + 4 * i
                t = [plan[0, at + k] for k in range(4)]
                got = [gather(n, t[k], at + k) for k in range(4)]
                for k in range(4):
                    settle(t[k], got[k])
                return 0

            lax.fori_loop(0, plan[1, len(CLASSES) + c], body, 0)

    @pl.when(wide)
    def _():
        for s in range(3):
            for g in range(0, 128, 32):
                xtab[s * 128 + g:s * 128 + g + 32] = three(*[xg[s, k, g:g + 32] for k in range(3)])
            for e, r in ((0, 7), (1, 0)):
                xtab[384 + 2 * s + e:385 + 2 * s + e] = three(*[xc[s, e, k, r:r + 1] for k in range(3)])
        xtab[390:] = jnp.zeros((10, 8, 128), f32)

        def tile(t, _):
            here = xtab[128 + t]
            for a in range(3):
                pa[a] = jnp.transpose(jnp.broadcast_to(here[a:a + 1], (128, 128)))

            def slot(s, total):
                g = named[s, t]
                q = xtab[g]
                dist = jnp.zeros((128, 128), f32)
                for a in range(3):
                    diff = pa[a] - q[a:a + 1]
                    dist = dist + diff * diff
                w = jnp.exp(dist * (-1.0 / 0.72))
                hi = w.astype(bf16)
                both = jnp.concatenate([hi, (w - hi.astype(f32)).astype(bf16)], axis=0)
                return total + lax.dot_general(vtab[g], both, NT, preferred_element_type=f32)

            settle(t, lax.fori_loop(0, 9, slot, jnp.zeros((16, 256), f32)))
            return 0

        lax.fori_loop(0, 128, tile, 0)

    got = sm[:, 0:128]
    out[...] = got
    spread[...] = jnp.sqrt(got * got + 0.01)


def run_smooth(vg, vc, xg, xc, cols0, cols1, cols2, feats, plan, named):
    vm, sm = pl.BlockSpec(memory_space=pltpu.VMEM), pl.BlockSpec(memory_space=pltpu.SMEM)
    return pl.pallas_call(
        smooth_kernel,
        out_shape=[jax.ShapeDtypeStruct((3, 128, 128), f32)] * 2,
        in_specs=[sm] * 2 + [vm] * 8,
        out_specs=[vm] * 2,
        scratch_shapes=[
            pltpu.VMEM((400, 16, 128), bf16), pltpu.VMEM((3, 136, 128), f32),
            pltpu.VMEM((400, 8, 128), f32), pltpu.VMEM((3, 128, 128), f32)],
        compiler_params=pltpu.CompilerParams(vmem_limit_bytes=VM2 * 2**20),
        name="smooth_tiles",
    )(plan, named, vg, vc, xg, xc, cols0, cols1, cols2, feats)


def total_kernel(cuts, spread, out, held, ss, rs):
    ev, cut = lax.axis_index("ev"), lax.axis_index("cuts")
    yh, inner = lax.div(ev, 8) * 8, lax.rem(ev, 8)
    steps = [[(yh + lax.rem(inner + d, 8), cut) for d in range(1, 8)]]
    low = min(4, cuts)
    base, lane = lax.div(cut, low) * low, lax.rem(cut, low)
    steps.append([(lax.rem(ev + 8 * a, 16), base + lax.rem(lane + b, low)) for a in (0, 1) for b in range(low) if a + b])
    if cuts > low:
        steps.append([(ev, lax.rem(cut + d * low, cuts)) for d in range(1, cuts // low)])
    barrier = pltpu.get_barrier_semaphore()
    n = 0
    for step in steps:
        for dev in step:
            pl.semaphore_signal(barrier, inc=1, device_id=dev, device_id_type=MESH)
            n += 1
    part = jnp.sum(spread[...].reshape(48, 8, 128), axis=0)
    held[0] = jnp.broadcast_to(jnp.sum(part, axis=(0, 1), keepdims=True), (1, 128))
    pl.semaphore_wait(barrier, n)
    slot, mine, copies = 1, 0, []
    for k, step in enumerate(steps):
        m = len(step)
        for d, dev in enumerate(step):
            c = pltpu.make_async_remote_copy(src_ref=held.at[mine], dst_ref=held.at[slot + d],
                                             send_sem=ss.at[slot + d], recv_sem=rs.at[slot + d], device_id=dev, device_id_type=MESH)
            c.start()
            copies.append(c)
        total = held[mine]
        for d in range(m):
            copies[-m + d].wait_recv()
        for d in range(m):
            total = total + held[slot + d]
        slot += m
        mine = slot
        held[mine] = total
        slot += 1
    everything = 3 * 16384 * 16 * cuts
    out[...] = held[mine, 0:1, 0:1] / everything / spread[...]
    for c in copies:
        c.wait_send()


def run_total(spread, cuts):
    vm = pl.BlockSpec(memory_space=pltpu.VMEM)
    dma = pltpu.SemaphoreType.DMA
    return pl.pallas_call(
        functools.partial(total_kernel, cuts),
        out_shape=jax.ShapeDtypeStruct((3, 128, 128), f32),
        in_specs=[vm], out_specs=vm,
        scratch_shapes=[pltpu.VMEM((32, 1, 128), f32), dma((32,)), dma((32,))],
        compiler_params=pltpu.CompilerParams(collective_id=1, has_side_effects=True, vmem_limit_bytes=8 * 2**20),
        name="sum_over_devices",
    )(spread)


def on_device(cuts, kernels, coords, neighbours):
    got = run_exchange(kernels.reshape(3, 2, 4, 2, 128, 128), coords.reshape(3, 128, 128), neighbours[0].T, cuts)
    smoothed, spread = run_smooth(*got)
    weights = run_total(spread, cuts)
    return smoothed.reshape(3, 1, 16384), weights.reshape(3, 1, 16384)


def solution(mesh):
    cuts = mesh.shape["cuts"]
    return jax.shard_map(
        functools.partial(on_device, cuts),
        mesh=mesh,
        in_specs=(P("ev", None, "cuts", None), P(None, "cuts", "ev"), P("cuts", "ev", None)),
        out_specs=(P(None, "cuts", "ev"), P(None, "cuts", "ev")),
        check_vma=False,
    )
```

```python
import functools
import jax
import jax.numpy as jnp
from jax import lax
from jax.experimental import pallas as pl
from jax.experimental.pallas import tpu as pltpu
from jax.sharding import PartitionSpec as P

MESH = pl.DeviceIdType.MESH
f32 = jnp.float32
bf16 = jnp.bfloat16
C2 = 1.4426950408889634 / 0.72
CLASSES = (9, 8, 7, 6, 5)
PLACES = 144
ZERO = 391
LIMIT = 1.5
SHIFT = C2 * 3.0 * LIMIT * LIMIT
NT = (((1,), (1,)), ((), ()))
VM1, VM2 = 16, 12
PIECES = ((0, 48, True), (48, 96, True), (96, 128, False))


def three(a, b, c):
    n = a.shape[0]
    row = lax.broadcasted_iota(jnp.int32, (1, 8, 128), 1)
    wide = lambda r: jnp.broadcast_to(r[:, None, :], (n, 8, 128))
    return jnp.where(row == 0, wide(a), jnp.where(row == 1, wide(b), wide(c)))


def plan_slots(nb, plan, named, reach):
    i32 = jnp.int32
    zero = jnp.zeros((1, 128), i32)
    count = zero
    found = [zero + ZERO for _ in range(9)]
    for s in range(9):
        v = nb[s:s + 1]
        row = jnp.where(v >= 260, 2, jnp.where(v >= 130, 1, 0))
        col = v - 130 * row
        spot = jnp.where(col == 0, 384 + 2 * row, jnp.where(col == 129, 385 + 2 * row, row * 128 + col - 1))
        for j in range(s + 1):
            found[j] = jnp.where((v >= 0) & (count == j), spot, found[j])
        count = count + jnp.where(v >= 0, 1, 0)
    named[...] = jnp.concatenate(found + [zero] * 7, axis=0)
    size = jnp.maximum(count, CLASSES[-1])
    member = jnp.concatenate([jnp.where(size == n, 1.0, 0.0) for n in CLASSES] + [jnp.zeros((3, 128), f32)], axis=0)
    upto = lax.broadcasted_iota(i32, (128, 128), 0) <= lax.broadcasted_iota(i32, (128, 128), 1)
    run = jnp.dot(member.astype(bf16), jnp.where(upto, 1.0, 0.0).astype(bf16), preferred_element_type=f32)
    lane = lax.broadcasted_iota(i32, (1, 256), 1)
    start = jnp.zeros((1, 1), f32)
    place = jnp.zeros((1, 128), f32)
    spans = jnp.where(lane == 12, jnp.where(reach <= LIMIT, 1.0, 0.0), 0.0)
    for c in range(len(CLASSES)):
        fours = jnp.floor((jnp.sum(member[c:c + 1], axis=1, keepdims=True) + 3.0) * 0.25)
        place = place + member[c:c + 1] * (start + run[c:c + 1] - 1.0)
        spans = spans + jnp.where(lane == c, start, 0.0) + jnp.where(lane == len(CLASSES) + c, fours, 0.0)
        start = start + 4.0 * fours
    hit = jnp.where(place.astype(i32) == lax.broadcasted_iota(i32, (256, 128), 0), 1.0, 0.0).astype(bf16)
    tile = lax.broadcasted_iota(i32, (8, 128), 1)
    what = jnp.where(lax.broadcasted_iota(i32, (8, 128), 0) == 0, tile - 128, 0).astype(f32).astype(bf16)
    order = lax.dot_general(what, hit, NT, preferred_element_type=f32)[0:1] + 128.0
    plan[...] = jnp.concatenate([order, spans, jnp.zeros((6, 256), f32)], axis=0).astype(i32)


def exchange(cuts, d, x_ref, nb, vg, vc, xg, xc, cols0, cols1, cols2, feats, plan, named,
             mine, other, x1, x2, yb, ybig, xtab, ctab, yown, named_s, plan_s, tmp_sem,
             loc_sem, s0, r0, s1, r1, s2, r2, s3, r3, sh, rh):
    ev = lax.axis_index("ev")
    cut = lax.axis_index("cuts")
    core = lax.rem(ev, 2)
    x = lax.rem(lax.div(ev, 2), 4)
    yh = lax.div(ev, 8)
    yl = lax.rem(cut, 2)

    def at(y_, x_, c_):
        return (y_ * 8 + x_ * 2 + c_, cut)

    xp, xm, xo = lax.rem(x + 1, 4), lax.rem(x + 3, 4), lax.rem(x + 2, 4)
    twin = at(yh, x, 1 - core)
    right, left = at(yh, xp, core), at(yh, xm, core)
    across = at(1 - yh, x, core)
    beside = (ev, cut + 1 - 2 * yl)
    ahead, behind = cut + 2 - 4 * yl, cut - 2 + 4 * yl
    ok_ahead = (ahead >= 0) & (ahead < cuts)
    ok_behind = (behind >= 0) & (behind < cuts)
    near, far = 2 - 2 * yl, 2 * yl
    rel = [(de, dc) for de in (-1, 1) for dc in (-1, 0, 1)]

    def exists(de, dc):
        ok = (ev + de >= 0) & (ev + de < 16)
        if dc:
            ok = ok & (cut + dc >= 0) & (cut + dc < cuts)
        return ok

    barrier = pltpu.get_barrier_semaphore()
    for dev in (twin, right, left, across, beside):
        pl.semaphore_signal(barrier, inc=1, device_id=dev, device_id_type=MESH)
    expect = 5
    for ok, c in ((ok_ahead, ahead), (ok_behind, behind)):
        @pl.when(ok)
        def _(c=c):
            pl.semaphore_signal(barrier, inc=1, device_id=(ev, c), device_id_type=MESH)
        expect = expect + ok.astype(jnp.int32)
    for de, dc in rel:
        @pl.when(exists(de, dc))
        def _(de=de, dc=dc):
            pl.semaphore_signal(barrier, inc=1, device_id=(ev + de, cut + dc), device_id_type=MESH)
        expect = expect + exists(de, dc).astype(jnp.int32)

    n = len(PIECES)
    rows = [pl.ds(a, b - a) for a, b, _ in PIECES]
    ha = [pl.ds(a, (b - a) // 2) for a, b, _ in PIECES]
    hb = [pl.ds(a + (b - a) // 2, (b - a) // 2) for a, b, _ in PIECES]
    hx = [pl.ds(a // 2, (b - a) // 2) for a, b, _ in PIECES]

    locs = []
    for p in range(n):
        c = pltpu.make_async_copy(d.at[:, :, :, core, rows[p]], mine.at[:, :, :, rows[p]], loc_sem.at[p])
        c.start()
        locs.append(c)
    pl.semaphore_wait(barrier, expect)

    def remote(src, dst, ss, rs, dev, start=True):
        c = pltpu.make_async_remote_copy(src_ref=src, dst_ref=dst, send_sem=ss, recv_sem=rs,
                                         device_id=dev, device_id_type=MESH)
        if start:
            c.start()
        return c

    order = [xo, xp, xm, x]
    c0 = {}
    for p in range(n):
        for i, xx in enumerate(order):
            c0[p, i] = remote(d.at[:, :, xx, 1 - core, rows[p]], other.at[:, :, xx, rows[p]],
                              s0.at[p * 4 + i], r0.at[p * 4 + i], twin)

    def lend(full, part, sem):
        return remote(full.at[1, :, part], full.at[far, :, part], sh.at[sem], rh.at[sem], beside, False)

    def pass_on(full, part, sem):
        return remote(full.at[near, :, part], full.at[far, :, part], sh.at[sem], rh.at[sem], (ev, ahead), False)

    def corners(full, small, base, act):
        for i, (de, dc) in enumerate(rel):
            c = remote(full.at[1, :, pl.ds(120 if de > 0 else 0, 8)], small.at[1 - dc, 0 if de > 0 else 1],
                       sh.at[base + i], rh.at[base + i], (ev + de, cut + dc), False)
            if act == "start":
                pl.when(exists(de, dc))(c.start)
            elif act == "send":
                pl.when(exists(de, dc))(c.wait_send)
            else:
                pl.when(exists(-de, -dc))(c.wait_recv)

    whole = pl.ds(0, 128)
    xg[1] = x_ref[...]
    lend(xg, whole, 12).start()
    corners(xg, xc, 6, "start")

    own = x_ref[...]
    low, high = jnp.min(own, axis=2, keepdims=True), jnp.max(own, axis=2, keepdims=True)
    mid = jnp.broadcast_to(0.5 * high + 0.5 * low, own.shape)
    yown[...] = own - mid
    for g in range(0, 128, 32):
        ctab[g:g + 32] = three(*[mid[k, g:g + 32] for k in range(3)])
        xtab[128 + g:160 + g] = three(*[own[k, g:g + 32] for k in range(3)])
    xtab[390:] = jnp.zeros((10, 8, 128), f32)
    plan_slots(nb[...], plan, named, jnp.max(0.5 * high - 0.5 * low, axis=(0, 1), keepdims=True)[0])
    local = [pltpu.make_async_copy(named, named_s, tmp_sem.at[0]), pltpu.make_async_copy(plan, plan_s, tmp_sem.at[1])]
    for c in local:
        c.start()
    for c in local:
        c.wait()

    def columns(i, _):
        for j in [6 * i + u for u in range(6)]:
            t = jnp.clip(plan_s[0, j], 0, 127)
            for k, c in enumerate((cols0, cols1, cols2)):
                c[j] = jnp.transpose(jnp.broadcast_to(yown[k, pl.ds(t, 1)], (128, 128)))
        return 0

    def features(i, _):
        for j in [2 * i + u for u in range(2)]:
            t = jnp.clip(plan_s[0, j], 0, 127)
            c = ctab[t]
            made = []
            for s in range(9):
                y = jnp.clip(xtab[jnp.clip(named_s[s, t], 0, 399)] - c, -1e4, 1e4)
                b = y * y
                made.append((y * (2 * C2), (b[0:1] + b[1:2] + b[2:3]) * (-C2) - SHIFT))
            for s, (y, b) in enumerate(made):
                feats[j * 9 + s] = y
                feats[j * 9 + s, 3:4] = b
        return 0

    def some_columns(i):
        lax.fori_loop(3 * i, 3 * i + 3, columns, 0)

    def neighbour_positions():
        pl.when(ok_behind)(pass_on(xg, whole, 13).wait_recv)
        corners(xg, xc, 6, "recv")
        for s in (0, 2):
            for g in range(0, 128, 32):
                xtab[s * 128 + g:s * 128 + g + 32] = three(*[xg[s, k, g:g + 32] for k in range(3)])
        for s in range(3):
            for e, r in ((0, 7), (1, 0)):
                xtab[384 + 2 * s + e:385 + 2 * s + e] = three(*[xc[s, e, k, r:r + 1] for k in range(3)])

    c1, c2, c3 = {}, {}, {}

    def arrive(p, xx, i):
        c0[p, i].wait_recv()
        mine[:, :, xx, rows[p]] += other[:, :, xx, rows[p]]

    def level(p, k):
        first = PIECES[p][2]
        if first:
            ys, step = slice(None), k
        else:
            ys, step = pl.ds(yh, 1), k - 1
        if k == 1:
            locs[p].wait()
            arrive(p, xo, 0)
            if not first:
                for i in (1, 2, 3):
                    arrive(p, order[i], i)
                c3[p] = remote(mine.at[:, 1 - yh, :, rows[p]], ybig.at[:, :, pl.ds(0, PIECES[p][1] - PIECES[p][0])], s3.at[p], r3.at[p], across)
        if k == 2 and not first:
            c3[p].wait_recv()
            mine[:, yh, :, rows[p]] += ybig[:, :, pl.ds(0, PIECES[p][1] - PIECES[p][0])]
        if step == 1:
            for side, half, dev in ((0, ha[p], right), (1, hb[p], left)):
                c1[p, side] = remote(mine.at[:, ys, xo, half], x1.at[side, :, ys, hx[p]], s1.at[2 * p + side], r1.at[2 * p + side], dev)
        elif step == 2:
            for side, xx, half, dev in ((0, xp, ha[p], right), (1, xm, hb[p], left)):
                if first:
                    arrive(p, xx, 1 + side)
                c1[p, side].wait_recv()
                mine[:, ys, xx, half] += x1[side, :, ys, hx[p]]
                c2[p, side] = remote(mine.at[:, ys, xx, rows[p]], x2.at[side, :, ys, rows[p]], s2.at[2 * p + side], r2.at[2 * p + side], dev)
        elif step == 3:
            if first:
                arrive(p, x, 3)
            for side in (0, 1):
                c2[p, side].wait_recv()
                mine[:, ys, x, rows[p]] += x2[side, :, ys, rows[p]]
            if first:
                c3[p] = remote(mine.at[:, 1 - yh, x, rows[p]], yb.at[:, rows[p]], s3.at[p], r3.at[p], across)
            else:
                vg[1, :, rows[p]] = mine[:, yh, x, rows[p]]
                lend(vg, rows[p], 14 + p).start()
        elif step == 4:
            c3[p].wait_recv()
            vg[1, :, rows[p]] = mine[:, yh, x, rows[p]] + yb[:, rows[p]]
            lend(vg, rows[p], 14 + p).start()

    some_columns(0)
    for p in range(n):
        level(p, 1)
    some_columns(1)
    lend(xg, whole, 12).wait_recv()
    pl.when(ok_ahead)(pass_on(xg, whole, 13).start)
    some_columns(2)
    for p in range(n):
        level(p, 2)
    some_columns(3)
    some_columns(4)
    for p in range(n):
        level(p, 3)
    some_columns(5)
    neighbour_positions()
    lax.fori_loop(0, PLACES // 4, features, 0)
    for p in range(n):
        level(p, 4)
    corners(vg, vc, 0, "start")
    some_columns(6)
    some_columns(7)
    for p in reversed(range(n)):
        lend(vg, rows[p], 14 + p).wait_recv()
        pl.when(ok_ahead)(pass_on(vg, rows[p], 14 + n + p).start)
    lax.fori_loop(PLACES // 4, PLACES // 2, features, 0)
    for p in range(n):
        pl.when(ok_behind)(pass_on(vg, rows[p], 14 + n + p).wait_recv)
    corners(vg, vc, 0, "recv")

    for c in list(c0.values()) + list(c1.values()) + list(c2.values()) + list(c3.values()):
        c.wait_send()
    lend(xg, whole, 12).wait_send()
    pl.when(ok_ahead)(pass_on(xg, whole, 13).wait_send)
    for p in range(n):
        lend(vg, rows[p], 14 + p).wait_send()
        pl.when(ok_ahead)(pass_on(vg, rows[p], 14 + n + p).wait_send)
    corners(xg, xc, 6, "send")
    corners(vg, vc, 0, "send")


def run_exchange(kern, coords, nb, cuts):
    n = len(PIECES)
    deep = max(b - a for a, b, first in PIECES if not first)
    vm = pl.BlockSpec(memory_space=pltpu.VMEM)
    dma = pltpu.SemaphoreType.DMA
    shape = jax.ShapeDtypeStruct
    return pl.pallas_call(
        functools.partial(exchange, cuts),
        out_shape=[shape((3, 3, 128, 128), f32), shape((3, 2, 3, 8, 128), f32),
                   shape((3, 3, 128, 128), f32), shape((3, 2, 3, 8, 128), f32),
                   *[shape((PLACES, 128, 128), f32)] * 3, shape((PLACES * 9, 8, 128), f32),
                   shape((8, 256), jnp.int32), shape((16, 128), jnp.int32)],
        in_specs=[pl.BlockSpec(memory_space=pltpu.HBM), vm, vm],
        out_specs=[vm] * 10,
        scratch_shapes=[
            pltpu.VMEM((3, 2, 4, 128, 128), f32), pltpu.VMEM((3, 2, 4, 128, 128), f32),
            pltpu.VMEM((2, 3, 2, 64, 128), f32), pltpu.VMEM((2, 3, 2, 128, 128), f32),
            pltpu.VMEM((3, 128, 128), f32), pltpu.VMEM((3, 4, deep, 128), f32),
            pltpu.VMEM((400, 8, 128), f32), pltpu.VMEM((128, 8, 128), f32), pltpu.VMEM((3, 128, 128), f32),
            pltpu.SMEM((16, 128), jnp.int32), pltpu.SMEM((8, 256), jnp.int32), dma((2,)),
            dma((n,)), dma((4 * n,)), dma((4 * n,)), dma((2 * n,)), dma((2 * n,)), dma((2 * n,)), dma((2 * n,)),
            dma((n,)), dma((n,)), dma((14 + 2 * n,)), dma((14 + 2 * n,))],
        compiler_params=pltpu.CompilerParams(collective_id=0, has_side_effects=True, vmem_limit_bytes=VM1 * 2**20),
        name="event_sum_and_halo",
    )(kern, coords, nb)


def smooth_kernel(plan, named, vg, vc, xg, xc, cols0, cols1, cols2, feats, out, spread, vtab, sm, xtab, pa):
    row8 = lax.broadcasted_iota(jnp.int32, (1, 8, 128), 1)

    def values(at, v):
        n = v.shape[0]
        v = jnp.where(row8 < 3, v, jnp.where(row8 == 3, 1.0, 0.0))
        hi = v.astype(bf16).astype(f32)
        vtab[at:at + n] = jnp.concatenate([hi, v - hi], axis=1).astype(bf16)

    for s in range(3):
        for g in range(0, 128, 32):
            values(s * 128 + g, three(*[vg[s, k, g:g + 32] for k in range(3)]))
        for e, r in ((0, 7), (1, 0)):
            values(384 + 2 * s + e, three(*[vc[s, e, k, r:r + 1] for k in range(3)]))
    vtab[390:] = jnp.zeros((10, 16, 128), bf16)

    def settle(t, r):
        total = r[:, :128] + r[:, 128:]
        mean = (total[0:3] + total[8:11]) / total[3:4]
        for k in range(3):
            sm[k, pl.ds(t, 1)] = mean[k:k + 1]

    def gather(n, t, j):
        tt = jnp.minimum(t, 127)
        col = [c[j] for c in (cols0, cols1, cols2)]
        total = None
        for a in range(0, n, 2):
            both, v = [], []
            for s in range(a, min(a + 2, n)):
                r = [jnp.broadcast_to(feats[j * 9 + s, k:k + 1], (128, 128)) for k in range(4)]
                w = jnp.exp2(((col[0] * r[0] + r[3]) + col[1] * r[1]) + col[2] * r[2])
                hi = w.astype(bf16)
                both.append(jnp.concatenate([hi, (w - hi.astype(f32)).astype(bf16)], axis=0))
                v.append(vtab[named[s, tt]])
            r = lax.dot_general(jnp.concatenate(v, axis=1), jnp.concatenate(both, axis=1), NT, preferred_element_type=f32)
            total = r if total is None else total + r
        return total

    wide = plan[1, 12] == 0

    @pl.when(jnp.logical_not(wide))
    def _():
        for c, n in enumerate(CLASSES):
            first = plan[1, c]

            def body(i, _, n=n, first=first):
                at = first + 4 * i
                t = [plan[0, at + k] for k in range(4)]
                got = [gather(n, t[k], at + k) for k in range(4)]
                for k in range(4):
                    settle(t[k], got[k])
                return 0

            lax.fori_loop(0, plan[1, len(CLASSES) + c], body, 0)

    @pl.when(wide)
    def _():
        for s in range(3):
            for g in range(0, 128, 32):
                xtab[s * 128 + g:s * 128 + g + 32] = three(*[xg[s, k, g:g + 32] for k in range(3)])
            for e, r in ((0, 7), (1, 0)):
                xtab[384 + 2 * s + e:385 + 2 * s + e] = three(*[xc[s, e, k, r:r + 1] for k in range(3)])
        xtab[390:] = jnp.zeros((10, 8, 128), f32)

        def tile(t, _):
            here = xtab[128 + t]
            for a in range(3):
                pa[a] = jnp.transpose(jnp.broadcast_to(here[a:a + 1], (128, 128)))

            def slot(s, total):
                g = named[s, t]
                q = xtab[g]
                dist = jnp.zeros((128, 128), f32)
                for a in range(3):
                    diff = pa[a] - q[a:a + 1]
                    dist = dist + diff * diff
                w = jnp.exp(dist * (-1.0 / 0.72))
                hi = w.astype(bf16)
                both = jnp.concatenate([hi, (w - hi.astype(f32)).astype(bf16)], axis=0)
                return total + lax.dot_general(vtab[g], both, NT, preferred_element_type=f32)

            settle(t, lax.fori_loop(0, 9, slot, jnp.zeros((16, 256), f32)))
            return 0

        lax.fori_loop(0, 128, tile, 0)

    got = sm[:, 0:128]
    out[...] = got
    spread[...] = jnp.sqrt(got * got + 0.01)


def run_smooth(vg, vc, xg, xc, cols0, cols1, cols2, feats, plan, named):
    vm, sm = pl.BlockSpec(memory_space=pltpu.VMEM), pl.BlockSpec(memory_space=pltpu.SMEM)
    return pl.pallas_call(
        smooth_kernel,
        out_shape=[jax.ShapeDtypeStruct((3, 128, 128), f32)] * 2,
        in_specs=[sm] * 2 + [vm] * 8,
        out_specs=[vm] * 2,
        scratch_shapes=[
            pltpu.VMEM((400, 16, 128), bf16), pltpu.VMEM((3, 136, 128), f32),
            pltpu.VMEM((400, 8, 128), f32), pltpu.VMEM((3, 128, 128), f32)],
        compiler_params=pltpu.CompilerParams(vmem_limit_bytes=VM2 * 2**20),
        name="smooth_tiles",
    )(plan, named, vg, vc, xg, xc, cols0, cols1, cols2, feats)


def total_kernel(cuts, spread, out, held, ss, rs):
    ev, cut = lax.axis_index("ev"), lax.axis_index("cuts")
    yh, inner = lax.div(ev, 8) * 8, lax.rem(ev, 8)
    steps = [[(yh + lax.rem(inner + d, 8), cut) for d in range(1, 8)]]
    low = min(4, cuts)
    base, lane = lax.div(cut, low) * low, lax.rem(cut, low)
    steps.append([(lax.rem(ev + 8 * a, 16), base + lax.rem(lane + b, low)) for a in (0, 1) for b in range(low) if a + b])
    if cuts > low:
        steps.append([(ev, lax.rem(cut + d * low, cuts)) for d in range(1, cuts // low)])
    barrier = pltpu.get_barrier_semaphore()
    n = 0
    for step in steps:
        for dev in step:
            pl.semaphore_signal(barrier, inc=1, device_id=dev, device_id_type=MESH)
            n += 1
    part = jnp.sum(spread[...].reshape(48, 8, 128), axis=0)
    held[0] = jnp.broadcast_to(jnp.sum(part, axis=(0, 1), keepdims=True), (1, 128))
    pl.semaphore_wait(barrier, n)
    slot, mine, copies = 1, 0, []
    for k, step in enumerate(steps):
        m = len(step)
        for d, dev in enumerate(step):
            c = pltpu.make_async_remote_copy(src_ref=held.at[mine], dst_ref=held.at[slot + d],
                                             send_sem=ss.at[slot + d], recv_sem=rs.at[slot + d], device_id=dev, device_id_type=MESH)
            c.start()
            copies.append(c)
        total = held[mine]
        for d in range(m):
            copies[-m + d].wait_recv()
        for d in range(m):
            total = total + held[slot + d]
        slot += m
        mine = slot
        held[mine] = total
        slot += 1
    everything = 3 * 16384 * 16 * cuts
    out[...] = held[mine, 0:1, 0:1] / everything / spread[...]
    for c in copies:
        c.wait_send()


def run_total(spread, cuts):
    vm = pl.BlockSpec(memory_space=pltpu.VMEM)
    dma = pltpu.SemaphoreType.DMA
    return pl.pallas_call(
        functools.partial(total_kernel, cuts),
        out_shape=jax.ShapeDtypeStruct((3, 128, 128), f32),
        in_specs=[vm], out_specs=vm,
        scratch_shapes=[pltpu.VMEM((32, 1, 128), f32), dma((32,)), dma((32,))],
        compiler_params=pltpu.CompilerParams(collective_id=1, has_side_effects=True, vmem_limit_bytes=8 * 2**20),
        name="sum_over_devices",
    )(spread)


def on_device(cuts, kernels, coords, neighbours):
    got = run_exchange(kernels.reshape(3, 2, 4, 2, 128, 128), coords.reshape(3, 128, 128), neighbours[0].T, cuts)
    smoothed, spread = run_smooth(*got)
    weights = run_total(spread, cuts)
    return smoothed.reshape(3, 1, 16384), weights.reshape(3, 1, 16384)


def solution(mesh):
    cuts = mesh.shape["cuts"]
    return jax.shard_map(
        functools.partial(on_device, cuts),
        mesh=mesh,
        in_specs=(P("ev", None, "cuts", None), P(None, "cuts", "ev"), P("cuts", "ev", None)),
        out_specs=(P(None, "cuts", "ev"), P(None, "cuts", "ev")),
        check_vma=False,
    )
```
